512 devices in a mesh: row: 32 (over y_lo, x, core), col: 16 (over y_hi, z).
Axes of the slice: x: 4, y: 8 (y_hi: 2, y_lo: 4; y = y_hi * 4 + y_lo), z: 8, core: 2. Of those that a mesh axis runs over, the one named last changes fastest.
Arguments:
- queries: bfloat16 [16384, 2048], P('row', 'col'), may hold values from -8 to 8
- keys: bfloat16 [16384, 512], P('row'), may hold values from -8 to 8
- values: bfloat16 [16384, 512], P('row'), may hold values from -6 to 6
- out_weight: bfloat16 [2048, 4096], P('col'), may hold values from -0.75 to 0.75
- slot_span: int32 [32], replicated, may hold values from 0 to 31, each once
Outputs:
- mixed: bfloat16 [16384, 4096], P('row', 'col')
The draws below stay inside these ranges and needn't reach their ends.
Inputs may be any that keep to these rules, and one draw needn't show every extreme that they name: `slot_span`: each of the 32 sequence blocks is stored in exactly one slot.
All inputs are finite; a program needn't handle non-finite values.
Results may differ from the reference program's by a relative error of at most 0.03.
Values may be sent and summed in bfloat16 or wider, within the bound.
A program may use at most 64 MiB of HBM per device.

```python
import math
import jax
import jax.numpy as jnp
from jax import lax

QUERY_HEADS = 16
KEY_VALUE_HEADS = 4
HEAD_SIZE = 128
D = 4096
TOK_DEV = 512
SEQUENCE_TOKENS = 16384
N_ROW = 32
N_COL = 16


def draw_queries(key, part):
    key = jax.random.fold_in(key, 11)
    base_offset = jnp.clip(jax.random.normal(key, (SEQUENCE_TOKENS, QUERY_HEADS * HEAD_SIZE), jnp.float32), -6.0, 6.0)
    return base_offset.astype(jnp.bfloat16)


def draw_keys(key, part):
    key = jax.random.fold_in(key, 23)
    base_offset = jnp.clip(jax.random.normal(key, (SEQUENCE_TOKENS, KEY_VALUE_HEADS * HEAD_SIZE), jnp.float32), -6.0, 6.0)
    return base_offset.astype(jnp.bfloat16)


def spiked(drawn, rng, source, target, shards_of, factor):
    owner, partner = [(jnp.arange(drawn.shape[position]) // (drawn.shape[position] // shards_of)).reshape([-1 if axis == position else 1 for axis in range(drawn.ndim)]) for position in (source, target)]
    chosen = jax.random.permutation(rng, shards_of)[partner]
    strong = (owner == chosen) | (owner == (partner + shards_of // 2) % shards_of)
    return jnp.where(strong, factor * drawn, drawn)


def shard_levels(rng, extent, shards, smallest, high):
    gain = 1.0
    for axis_at, parts in shards:
        heights = jax.random.uniform(jax.random.fold_in(jax.random.fold_in(rng, 6), axis_at), (parts,), jnp.float32, smallest / len(shards), high / len(shards))
        gain = gain * jnp.repeat(jnp.exp(heights), extent[axis_at] // parts).reshape((-1,) + (1,) * (len(extent) - 1 - axis_at))
    return gain


def normal_values(own_key, extent, deviation, reach, split=(), held_as=jnp.bfloat16):
    values = deviation * jax.random.normal(own_key, extent, jnp.float32)
    if split:
        values = values * shard_levels(own_key, extent, split, -0.22, 0.18)
    return jnp.clip(values, -reach, reach).astype(held_as)


def noise_with(rng, dims, deviation, bound, cuts, heavy, held_as=jnp.bfloat16):
    values = deviation * jax.random.normal(rng, dims, jnp.float32)
    if cuts:
        values = values * shard_levels(rng, dims, cuts, -0.22, 0.18)
    return jnp.clip(spiked(values, jax.random.fold_in(rng, 3), *heavy), -bound, bound).astype(held_as)


def setup_inputs(seed: int = 0) -> dict:
    arg_keys = jax.random.split(jax.random.key(seed), 6)
    queries = draw_queries(jax.random.fold_in(arg_keys[5], 71), 0)
    keys = draw_keys(jax.random.fold_in(arg_keys[5], 71), 0)
    values = normal_values(arg_keys[2], (SEQUENCE_TOKENS, KEY_VALUE_HEADS * HEAD_SIZE), 1.0, 6.0, ((0, 32),))
    out_weight = noise_with(arg_keys[3], (QUERY_HEADS * HEAD_SIZE, D), HEAD_SIZE ** -0.5, 0.75, ((0, 16),), (0, 1, 16, 2.0))
    slot_span = jax.random.permutation(arg_keys[4], N_ROW).astype(jnp.int32)
    return {"queries": queries, "keys": keys, "values": values, "out_weight": out_weight, "slot_span": slot_span}


def reference(queries, keys, values, out_weight, slot_span):
    rows = jnp.arange(SEQUENCE_TOKENS, dtype=jnp.int32)
    pos = (slot_span[rows // TOK_DEV] * TOK_DEV + rows % TOK_DEV).astype(jnp.int32)
    query_head_rows = queries.reshape(SEQUENCE_TOKENS, KEY_VALUE_HEADS, QUERY_HEADS // KEY_VALUE_HEADS, HEAD_SIZE)
    key_head_rows = keys.reshape(SEQUENCE_TOKENS, KEY_VALUE_HEADS, HEAD_SIZE).astype(jnp.float32)
    value_head_rows = values.reshape(SEQUENCE_TOKENS, KEY_VALUE_HEADS, HEAD_SIZE).astype(jnp.float32)
    heads_dev = QUERY_HEADS // N_COL
    weight_parts = out_weight.astype(jnp.float32).reshape(N_COL, heads_dev * HEAD_SIZE, D)
    scale = HEAD_SIZE ** -0.5
    width = math.gcd(SEQUENCE_TOKENS, 256)

    def one_block(start):
        block = lax.dynamic_slice_in_dim(query_head_rows, start, width, 0).astype(jnp.float32)
        block_pos = lax.dynamic_slice_in_dim(pos, start, width, 0)
        scores = jnp.einsum("qkgd,skd->kgqs", block, key_head_rows) * scale
        visible = (pos[None, :] <= block_pos[:, None])[None, None]
        scores = jnp.where(visible, scores, jnp.float32(-1e30))
        peak = jnp.max(scores, axis=-1)
        weights = jnp.where(visible, jnp.exp(scores - peak[..., None]), jnp.float32(0.0)).astype(jnp.bfloat16)
        total = jnp.sum(weights.astype(jnp.float32), axis=-1)
        summed = jnp.einsum("kgqs,skd->qkgd", weights.astype(jnp.float32), value_head_rows)
        total = jnp.transpose(total, (2, 0, 1))[..., None]
        attended = (summed / total).astype(jnp.bfloat16).reshape(width, N_COL, heads_dev * HEAD_SIZE)
        pieces = jnp.einsum("qch,chd->cqd", attended.astype(jnp.float32), weight_parts, precision=lax.Precision.HIGHEST)
        pieces = lax.optimization_barrier(pieces.astype(jnp.bfloat16)).astype(jnp.float32)
        return jnp.sum(pieces, axis=0).astype(jnp.bfloat16)

    starts = jnp.arange(SEQUENCE_TOKENS // width, dtype=jnp.int32) * width
    return lax.map(one_block, starts).reshape(SEQUENCE_TOKENS, D)
```

```python
import math

import jax
import jax.numpy as jnp
from jax import lax
from jax.experimental import pallas as pl
from jax.experimental.pallas import tpu as pltpu
from jax.sharding import PartitionSpec as P

MESH = pl.DeviceIdType.MESH
TOK = 512
HALF = TOK // 2
HEAD = 128
NX, NY, NZ = 4, 8, 8
OUT = 256
ROWS = 128
NB = TOK // ROWS
FLOOR = -1e30
HIDDEN = 3e30
SCALE = HEAD**-0.5 * math.log2(math.e)

FIRST = ((0, 0), (1, 0))
GROUPS = (
    ((0, 3), (0, 1), (3, 0)),
    ((1, 3), (1, 1), (2, 0), (0, 2)),
    ((3, 3), (3, 1), (1, 2)),
    ((2, 3), (2, 1), (3, 2)),
    ((2, 2),),
)
COPIES = 128


def kernel(
    span, queries, keys, values, weight, out,
    qbuf, kbuf, vbuf, wbuf, acc, peak, around, give, got, give_stat, got_stat, own_part, swap, swapped,
    send_sem, recv_sem, local_sem,
):
    row, col = lax.axis_index("row"), lax.axis_index("col")
    core, x, ylo = row % 2, (row // 2) % NX, row // (2 * NX)
    z, yhi = col % NZ, col // NZ
    y = yhi * 4 + ylo
    parity = y % 2
    toward = 1 - 2 * parity

    def device(xx, yy, zz, cc):
        xx, yy, zz = (xx + NX) % NX, (yy + NY) % NY, (zz + NZ) % NZ
        return (((yy % 4) * NX + xx) * 2 + cc, (yy // 4) * NZ + zz)

    def slot_row(yx, dx, dc):
        yy = (ylo // 2 + yx // 2) % 2 * 2 + (ylo + yx) % 2
        return (yy * NX + (x + dx) % NX) * 2 + (core + dc) % 2

    def at_y(dy):
        return device(x, y + dy, z, core)

    def at_x(dx):
        return device(x + dx, y, z, core)

    def at_z(dz):
        return device(x, y, z + dz, core)

    sibling = device(x, y, z, (core + 1) % 2)
    opposite = device(x, y + 4, z, core)

    barrier = pltpu.get_barrier_semaphore()
    peers = [at_y(toward), at_y(-toward), at_y(2), at_y(-2), opposite, at_x(1), at_x(-1), sibling]
    peers += [at_z(d) for d in range(1, NZ)]
    for peer in peers:
        pl.semaphore_signal(barrier, inc=1, device_id=peer, device_id_type=MESH)

    vbuf[:, :, :, :, HEAD:] = jnp.ones((4, NX, 2, HALF, HEAD), jnp.bfloat16)

    def tokens(ref, yy):
        yy = (yy + NY) % NY
        group = (yy // 4) * 2 + z // 4
        start = pl.multiple_of((yy % 2) * HALF, HALF)
        return ref.at[pl.ds(start, HALF), pl.ds(pl.multiple_of(group * HEAD, HEAD), HEAD)]

    def kslot(yx, dx, dc=0):
        return kbuf.at[yx, dx, dc]

    def vslot(yx, dx, dc=0):
        return vbuf.at[yx, dx, dc, :, pl.ds(0, HEAD)]

    own_weight = pl.ds(pl.multiple_of(col * OUT, OUT), OUT)
    other_weight = pl.ds(pl.multiple_of((1 - yhi) * (NZ * OUT) + z * OUT, OUT), OUT)
    here = [
        pltpu.make_async_copy(tokens(keys, y), kslot(0, 0), local_sem.at[0]),
        pltpu.make_async_copy(tokens(values, y), vslot(0, 0), local_sem.at[1]),
        pltpu.make_async_copy(queries, qbuf.at[pl.ds(0, TOK)], local_sem.at[2]),
        pltpu.make_async_copy(weight.at[:, own_weight], wbuf.at[pl.ds(0, HEAD), pl.ds(0, OUT)], local_sem.at[3]),
        pltpu.make_async_copy(weight.at[:, other_weight], wbuf.at[pl.ds(0, HEAD), pl.ds(OUT, OUT)], local_sem.at[4]),
    ]
    for copy in here:
        copy.start()
    pl.semaphore_wait(barrier, len(peers))

    started = []

    def push(src, dst, to):
        k = len(started)
        copy = pltpu.make_async_remote_copy(
            src_ref=src, dst_ref=dst, send_sem=send_sem.at[k], recv_sem=recv_sem.at[k], device_id=to, device_id_type=MESH
        )
        copy.start()
        started.append(copy)
        return copy

    arriving = {}

    def push_k(src, yx, dx, dc, to):
        arriving[yx, dx, dc, 0] = push(src, kslot(yx, dx, dc), to)

    def push_v(src, yx, dx, dc, to):
        arriving[yx, dx, dc, 1] = push(src, vslot(yx, dx, dc), to)

    def landed(yx, dx, dc):
        arriving[yx, dx, dc, 0].wait_recv()
        arriving[yx, dx, dc, 1].wait_recv()

    def across(yx, dx):
        push_k(kslot(yx, dx), yx, dx, 1, sibling)
        push_v(vslot(yx, dx), yx, dx, 1, sibling)

    def along_x(yx, k, v):
        push_k(k, yx, 3, 0, at_x(1))
        push_k(k, yx, 1, 0, at_x(-1))
        push_v(v, yx, 3, 0, at_x(1))
        push_v(v, yx, 1, 0, at_x(-1))

    def from_y(yx):
        landed(yx, 0, 0)
        along_x(yx, kslot(yx, 0), vslot(yx, 0))
        across(yx, 0)

    def from_x(yx):
        landed(yx, 3, 0)
        push_k(kslot(yx, 3), yx, 2, 0, at_x(1))
        across(yx, 3)
        landed(yx, 1, 0)
        push_v(vslot(yx, 1), yx, 2, 0, at_x(-1))
        across(yx, 1)

    def from_far(yx):
        landed(yx, 2, 0)
        across(yx, 2)

    def both(yx, dx):
        landed(yx, dx, 1)

    ask = push(queries, qbuf.at[pl.ds(TOK, TOK)], at_y(toward))
    push_k(tokens(keys, y + toward), 1, 0, 0, at_y(toward))
    push_k(tokens(keys, y - toward), 3, 0, 0, at_y(-toward))
    push_v(tokens(values, y + toward), 1, 0, 0, at_y(toward))
    push_v(tokens(values, y - toward), 3, 0, 0, at_y(-toward))
    along_x(0, tokens(keys, y), tokens(values, y))
    push_k(tokens(keys, y), 0, 0, 1, sibling)
    push_v(tokens(values, y), 0, 0, 1, sibling)
    push_k(tokens(keys, y + 2), 2, 0, 0, at_y(2))
    push_v(tokens(values, y - 2), 2, 0, 0, at_y(-2))
    half_rows = pl.multiple_of(core * (HEAD // 2), HEAD // 2)
    weights = []
    for d in range(1, NZ):
        zz = (z + d) % NZ
        for part, hi in ((0, yhi), (1, 1 - yhi)):
            columns = pl.ds(pl.multiple_of((hi * NZ + zz) * OUT, OUT), OUT)
            weights.append(
                push(
                    weight.at[pl.ds(half_rows, HEAD // 2), columns],
                    wbuf.at[pl.ds(d * HEAD + half_rows, HEAD // 2), pl.ds(part * OUT, OUT)],
                    at_z(d),
                )
            )
    for copy in here:
        copy.wait()

    my_span = (span[row], span[slot_row(1, 0, 0)])

    def hide(side, yx, dx, dc):
        return jnp.where(span[slot_row(yx, dx, dc)] < my_span[side], 0.0, HIDDEN).astype(jnp.float32)

    def step(group, side, block, first=False):
        at = pl.ds(side * TOK + block * ROWS, ROWS)
        query = qbuf[at, :]
        parts, top = [], None
        for yx, dx in group:
            k = kbuf[yx, dx].reshape(TOK, HEAD)
            scores = lax.dot_general(query, k, (((1,), (1,)), ((), ())), preferred_element_type=jnp.float32)
            for dc in range(2):
                part = scores[:, dc * HALF : (dc + 1) * HALF]
                seen = None
                if first and dc == 0 and (yx, side) in ((0, 0), (1, 1)):
                    i = lax.broadcasted_iota(jnp.int32, (ROWS, HALF), 0) + block * ROWS
                    j = lax.broadcasted_iota(jnp.int32, (ROWS, HALF), 1) + parity * HALF
                    seen = j <= i
                    hidden = None
                    shown = jnp.where(seen, part, jnp.float32(-HIDDEN))
                    part_top = jnp.maximum(shown[:, :HEAD], shown[:, HEAD:])
                else:
                    hidden = hide(side, yx, dx, dc)
                    part_top = jnp.maximum(part[:, :HEAD], part[:, HEAD:]) - hidden
                top = part_top if top is None else jnp.maximum(top, part_top)
                parts.append((part, hidden, seen))
        new = jnp.max(top, axis=1, keepdims=True) * SCALE
        if first:
            new = jnp.maximum(new, jnp.float32(FLOOR))
        else:
            old = peak[at, :]
            new = jnp.maximum(old, new)
            keep = jnp.exp2(old - new)[:, :1]
        new = jnp.broadcast_to(new, (ROWS, HEAD))
        total = None
        for n, (yx, dx) in enumerate(group):
            shares = []
            for part, hidden, seen in parts[2 * n : 2 * n + 2]:
                if seen is None:
                    power = part * SCALE - (new + hidden)[:, :1]
                else:
                    power = jnp.where(seen, part * SCALE - new[:, :1], jnp.float32(-HIDDEN))
                shares.append(jnp.exp2(power).astype(jnp.bfloat16))
            share = jnp.concatenate(shares, axis=1)
            value = vbuf[yx, dx].reshape(TOK, 2 * HEAD)
            term = jnp.dot(share, value, preferred_element_type=jnp.float32)
            total = term if total is None else total + term
        peak[at, :] = new
        acc[at, :] = total if first else acc[at, :] * keep + total

    def work(group, side, first=False):
        for block in range(NB):
            step(group, side, block, first)

    from_y(1)
    from_y(3)
    both(0, 0)
    ask.wait_recv()
    both(1, 0)
    work(FIRST, 0, True)
    from_x(0)
    work(FIRST, 1, True)
    from_y(2)
    for pair in GROUPS[0]:
        both(*pair)
    work(GROUPS[0], 0)
    from_x(1)
    work(GROUPS[0], 1)
    from_far(0)
    for pair in GROUPS[1]:
        both(*pair)
    work(GROUPS[1], 0)
    from_x(3)
    work(GROUPS[1], 1)
    from_far(1)
    for pair in GROUPS[2]:
        both(*pair)
    work(GROUPS[2], 0)
    from_x(2)
    work(GROUPS[2], 1)
    for copy in weights:
        copy.wait_recv()
    across_rows = [wbuf.at[pl.ds(d * HEAD + half_rows, HEAD // 2)] for d in range(1, NZ)]
    weights = [push(rows, rows, sibling) for rows in across_rows]
    from_far(3)
    for pair in GROUPS[3]:
        both(*pair)
    work(GROUPS[3], 0)
    from_far(2)
    work(GROUPS[3], 1)
    both(2, 2)

    given = []
    lane = lax.broadcasted_iota(jnp.int32, (ROWS, HEAD), 1)
    for block in range(NB):
        step(GROUPS[4], 1, block)
        at = pl.ds(TOK + block * ROWS, ROWS)
        here_rows = pl.ds(block * ROWS, ROWS)
        give[here_rows, :] = acc[at, :HEAD].astype(jnp.bfloat16)
        stat = jnp.where(lane == 0, peak[at, :], acc[at, HEAD:])
        give_stat[block] = stat.T[:8, :]
        given.append(
            (
                push(give.at[here_rows], got.at[here_rows], at_y(toward)),
                push(give_stat.at[block], got_stat.at[block], at_y(toward)),
            )
        )
    work(GROUPS[4], 0)

    rings = {}

    def cut(block, d):
        return around.at[pl.ds(block * ROWS, ROWS), pl.ds(d * HEAD, HEAD)]

    def send_z(block, d, to):
        src = (d - 1) if to == 1 else (d + 1) % NZ
        rings[block, d] = push(cut(block, src), cut(block, d), at_z(to))

    def combine(block):
        rows = pl.ds(block * ROWS, ROWS)
        for copy in given[block]:
            copy.wait_recv()
        stat = jnp.concatenate([got_stat[block], jnp.zeros((ROWS - 8, HEAD), jnp.float32)], axis=0).T
        peak_two, sum_two = stat[:, 0:1], stat[:, 1:2]
        peak_one, sum_one = peak[rows, :][:, :1], acc[rows, HEAD:][:, :1]
        top = jnp.maximum(peak_one, peak_two)
        one, two = jnp.exp2(peak_one - top), jnp.exp2(peak_two - top)
        total = acc[rows, :HEAD] * one + got[rows, :].astype(jnp.float32) * two
        around[rows, pl.ds(0, HEAD)] = (total / (sum_one * one + sum_two * two)).astype(jnp.bfloat16)
        send_z(block, 1, 1)
        send_z(block, NZ - 1, -1)

    def onward(block, stage):
        rings[block, stage].wait_recv()
        if stage < 3 or block % 2 == 0:
            send_z(block, stage + 1, 1)
        rings[block, NZ - stage].wait_recv()
        if stage < 3 or block % 2 == 1:
            send_z(block, NZ - stage - 1, -1)

    swaps = []

    def project(block):
        rings[block, 4].wait_recv()
        rows = pl.ds(block * ROWS, ROWS)
        part = jnp.dot(around[rows, :], wbuf[...], preferred_element_type=jnp.float32)
        own_part[rows, :] = part[:, :OUT]
        swap[rows, :] = part[:, OUT:].astype(jnp.bfloat16)
        swaps.append(push(swap.at[rows], swapped.at[rows], opposite))

    for turn in range(NB + 4):
        if turn < NB:
            combine(turn)
        if turn == 0:
            for copy in weights:
                copy.wait_recv()
        for stage in range(1, 5):
            block = turn - stage
            if 0 <= block < NB:
                if stage < 4:
                    onward(block, stage)
                else:
                    project(block)
    for block in range(NB):
        rows = pl.ds(block * ROWS, ROWS)
        swaps[block].wait_recv()
        out[rows, :] = (own_part[rows, :] + swapped[rows, :].astype(jnp.float32)).astype(jnp.bfloat16)
    for copy in started:
        copy.wait_send()


def local(queries, keys, values, out_weight, slot_span):
    vmem, anywhere = pl.BlockSpec(memory_space=pltpu.VMEM), pl.BlockSpec(memory_space=pl.ANY)
    return pl.pallas_call(
        kernel,
        out_shape=jax.ShapeDtypeStruct((TOK, OUT), jnp.bfloat16),
        in_specs=[pl.BlockSpec(memory_space=pltpu.SMEM), vmem, vmem, vmem, anywhere],
        out_specs=vmem,
        scratch_shapes=[
            pltpu.VMEM((2 * TOK, HEAD), jnp.bfloat16),
            pltpu.VMEM((4, NX, 2, HALF, HEAD), jnp.bfloat16),
            pltpu.VMEM((4, NX, 2, HALF, 2 * HEAD), jnp.bfloat16),
            pltpu.VMEM((NZ * HEAD, 2 * OUT), jnp.bfloat16),
            pltpu.VMEM((2 * TOK, 2 * HEAD), jnp.float32),
            pltpu.VMEM((2 * TOK, HEAD), jnp.float32),
            pltpu.VMEM((TOK, NZ * HEAD), jnp.bfloat16),
            pltpu.VMEM((TOK, HEAD), jnp.bfloat16),
            pltpu.VMEM((TOK, HEAD), jnp.bfloat16),
            pltpu.VMEM((NB, 8, ROWS), jnp.float32),
            pltpu.VMEM((NB, 8, ROWS), jnp.float32),
            pltpu.VMEM((TOK, OUT), jnp.float32),
            pltpu.VMEM((TOK, OUT), jnp.bfloat16),
            pltpu.VMEM((TOK, OUT), jnp.bfloat16),
            pltpu.SemaphoreType.DMA((COPIES,)),
            pltpu.SemaphoreType.DMA((COPIES,)),
            pltpu.SemaphoreType.DMA((5,)),
        ],
        compiler_params=pltpu.CompilerParams(
            collective_id=0, has_side_effects=True, vmem_limit_bytes=56 * 2**20
        ),
        cost_estimate=pl.CostEstimate(flops=9 * 10**9, bytes_accessed=3 * 10**6, transcendentals=9 * 10**6),
        name="attend_and_project",
    )(slot_span, queries, keys, values, out_weight)


def solution(mesh):
    in_specs = (P("row", "col"), P("row", None), P("row", None), P("col", None), P())
    return jax.shard_map(local, mesh=mesh, in_specs=in_specs, out_specs=P("row", "col"), check_vma=False)
```

```python
import math

import jax
import jax.numpy as jnp
from jax import lax
from jax.experimental import pallas as pl
from jax.experimental.pallas import tpu as pltpu
from jax.sharding import PartitionSpec as P

MESH = pl.DeviceIdType.MESH
TOK = 512
HALF = TOK // 2
HEAD = 128
NX, NY, NZ = 4, 8, 8
OUT = 256
ROWS = 256
STAT = 128
NB = TOK // ROWS
FLOOR = -1e30
HIDDEN = 3e30
SCALE = HEAD**-0.5 * math.log2(math.e)

LAST = ((2, 2),)
COPIES = 180
CUTS = 4
CUT = TOK // CUTS
LAG = 1
DIRECT = ()
TURNS = [(cut, stage) for stage in range(5) for cut in range(CUTS)]


def kernel(
    span, queries, keys, values, weight, out,
    qbuf, kbuf, vbuf, wbuf, acc, peak, around, give, got, give_stat, got_stat, own_part, swap, swapped,
    send_sem, recv_sem, local_sem,
):
    row, col = lax.axis_index("row"), lax.axis_index("col")
    core, x, ylo = row % 2, (row // 2) % NX, row // (2 * NX)
    z, yhi = col % NZ, col // NZ
    y = yhi * 4 + ylo
    parity = y % 2
    toward = 1 - 2 * parity

    def device(xx, yy, zz, cc):
        xx, yy, zz = (xx + NX) % NX, (yy + NY) % NY, (zz + NZ) % NZ
        return (((yy % 4) * NX + xx) * 2 + cc, (yy // 4) * NZ + zz)

    def slot_row(yx, dx, dc):
        yy = (ylo // 2 + yx // 2) % 2 * 2 + (ylo + yx) % 2
        return (yy * NX + (x + dx) % NX) * 2 + (core + dc) % 2

    def at_y(dy):
        return device(x, y + dy, z, core)

    def at_x(dx):
        return device(x + dx, y, z, core)

    def at_z(dz):
        return device(x, y, z + dz, core)

    sibling = device(x, y, z, (core + 1) % 2)
    opposite = device(x, y + 4, z, core)

    barrier = pltpu.get_barrier_semaphore()
    peers = [at_y(toward), at_y(-toward), at_y(2), at_y(-2), opposite, at_x(1), at_x(-1), at_x(2), sibling]
    peers += [at_z(d) for d in range(1, NZ)]
    for peer in peers:
        pl.semaphore_signal(barrier, inc=1, device_id=peer, device_id_type=MESH)

    vbuf[:, :, :, :, HEAD:] = jnp.ones((4, NX, 2, HALF, HEAD), jnp.bfloat16)

    def tokens(ref, yy):
        yy = (yy + NY) % NY
        group = (yy // 4) * 2 + z // 4
        start = pl.multiple_of((yy % 2) * HALF, HALF)
        return ref.at[pl.ds(start, HALF), pl.ds(pl.multiple_of(group * HEAD, HEAD), HEAD)]

    def kslot(yx, dx, dc=0):
        return kbuf.at[yx, dx, dc]

    def vslot(yx, dx, dc=0):
        return vbuf.at[yx, dx, dc, :, pl.ds(0, HEAD)]

    own_weight = pl.ds(pl.multiple_of(col * OUT, OUT), OUT)
    other_weight = pl.ds(pl.multiple_of((1 - yhi) * (NZ * OUT) + z * OUT, OUT), OUT)
    here = [
        pltpu.make_async_copy(tokens(keys, y), kslot(0, 0), local_sem.at[0]),
        pltpu.make_async_copy(tokens(values, y), vslot(0, 0), local_sem.at[1]),
        pltpu.make_async_copy(queries, qbuf.at[pl.ds(0, TOK)], local_sem.at[2]),
        pltpu.make_async_copy(weight.at[:, own_weight], wbuf.at[pl.ds(0, HEAD), pl.ds(0, OUT)], local_sem.at[3]),
        pltpu.make_async_copy(weight.at[:, other_weight], wbuf.at[pl.ds(0, HEAD), pl.ds(OUT, OUT)], local_sem.at[4]),
    ]
    for copy in here:
        copy.start()
    pl.semaphore_wait(barrier, len(peers))

    started = []

    def push(src, dst, to):
        k = len(started)
        copy = pltpu.make_async_remote_copy(
            src_ref=src, dst_ref=dst, send_sem=send_sem.at[k], recv_sem=recv_sem.at[k], device_id=to, device_id_type=MESH
        )
        copy.start()
        started.append(copy)
        return copy

    arriving = {}

    def push_k(src, yx, dx, dc, to):
        arriving[yx, dx, dc, 0] = push(src, kslot(yx, dx, dc), to)

    def push_v(src, yx, dx, dc, to):
        arriving[yx, dx, dc, 1] = push(src, vslot(yx, dx, dc), to)

    def landed(yx, dx, dc):
        arriving[yx, dx, dc, 0].wait_recv()
        arriving[yx, dx, dc, 1].wait_recv()

    def across(yx, dx):
        push_k(kslot(yx, dx), yx, dx, 1, sibling)
        push_v(vslot(yx, dx), yx, dx, 1, sibling)

    def along_x(yx, k, v):
        push_k(k, yx, 3, 0, at_x(1))
        push_k(k, yx, 1, 0, at_x(-1))
        push_v(v, yx, 3, 0, at_x(1))
        push_v(v, yx, 1, 0, at_x(-1))

    def both(yx, dx):
        landed(yx, dx, 1)

    push_k(tokens(keys, y + toward), 1, 0, 0, at_y(toward))
    push_k(tokens(keys, y - toward), 3, 0, 0, at_y(-toward))
    push_k(tokens(keys, y), 0, 0, 1, sibling)
    push_k(tokens(keys, y), 0, 3, 0, at_x(1))
    push_k(tokens(keys, y), 0, 1, 0, at_x(-1))
    push_v(tokens(values, y + toward), 1, 0, 0, at_y(toward))
    push_v(tokens(values, y - toward), 3, 0, 0, at_y(-toward))
    push_v(tokens(values, y), 0, 0, 1, sibling)
    push_v(tokens(values, y), 0, 3, 0, at_x(1))
    push_v(tokens(values, y), 0, 1, 0, at_x(-1))
    push_k(tokens(keys, y), 0, 2, 0, at_x(2))
    push_v(tokens(values, y), 0, 2, 0, at_x(-2))
    for copy in here:
        copy.wait()

    my_span = (span[row], span[slot_row(1, 0, 0)])

    def hide(side, yx, dx, dc):
        return jnp.where(span[slot_row(yx, dx, dc)] < my_span[side], 0.0, HIDDEN).astype(jnp.float32)

    def at_block(side, block):
        return pl.ds(side * TOK + block * ROWS, ROWS)

    def score(group, side, block):
        query = qbuf[at_block(side, block), :]
        return [
            lax.dot_general(
                query, kbuf[yx, dx].reshape(TOK, HEAD), (((1,), (1,)), ((), ())), preferred_element_type=jnp.float32
            )
            for yx, dx in group
        ]

    def soften(group, side, block, scores, first):
        at = at_block(side, block)
        parts, top = [], None
        for (yx, dx), whole in zip(group, scores):
            for dc in range(2):
                if first and dc == 0 and (yx, side) in ((0, 0), (1, 1)):
                    i = lax.broadcasted_iota(jnp.int32, (ROWS, HEAD), 0) + block * ROWS
                    j = lax.broadcasted_iota(jnp.int32, (ROWS, HEAD), 1) + parity * HALF
                    seen, hidden = i - j, None
                else:
                    seen, hidden = None, hide(side, yx, dx, dc)
                pair = []
                for c in range(2):
                    part = whole[:, dc * HALF + c * HEAD : dc * HALF + (c + 1) * HEAD]
                    if seen is not None:
                        part = jnp.where(seen >= c * HEAD, part, jnp.float32(-HIDDEN))
                    pair.append(part)
                part_top = jnp.maximum(*pair)
                if hidden is not None:
                    part_top = part_top - hidden
                top = part_top if top is None else jnp.maximum(top, part_top)
                parts.append((pair, hidden))
        new = jnp.broadcast_to(jnp.max(top, axis=1, keepdims=True) * SCALE, (ROWS, HEAD))
        keep = None
        if first:
            new = jnp.maximum(new, jnp.float32(FLOOR))
        else:
            old = peak[at, :]
            new = jnp.maximum(old, new)
            keep = jnp.exp2(old - new)
        peak[at, :] = new
        shares = []
        for pair, hidden in parts:
            base = new if hidden is None else new + hidden
            shares += [jnp.exp2(part * SCALE - base).astype(jnp.bfloat16) for part in pair]
        return keep, shares

    def gather_in(group, side, block, keep, shares):
        at = at_block(side, block)
        total = None
        for n, (yx, dx) in enumerate(group):
            share = jnp.concatenate(shares[4 * n : 4 * n + 4], axis=1)
            value = vbuf[yx, dx].reshape(TOK, 2 * HEAD)
            term = jnp.dot(share, value, preferred_element_type=jnp.float32)
            total = term if total is None else total + term
        if keep is None:
            acc[at, :] = total
        else:
            acc[at, :HEAD] = acc[at, :HEAD] * keep + total[:, :HEAD]
            acc[at, HEAD:] = acc[at, HEAD:] * keep + total[:, HEAD:]

    def work(group, sides, first=False, after=None):
        blocks = [(side, block) for side in sides for block in range(NB)]
        scores = score(group, *blocks[0])
        for n, (side, block) in enumerate(blocks):
            later = score(group, *blocks[n + 1]) if n + 1 < len(blocks) else None
            gather_in(group, side, block, *soften(group, side, block, scores, first))
            scores = later
            if after is not None:
                after(side, block)

    half_rows = pl.multiple_of(core * (HEAD // 2), HEAD // 2)
    weights = []

    def send_weights():
        for d in range(1, NZ):
            zz = (z + d) % NZ
            for part, hi in ((0, yhi), (1, 1 - yhi)):
                columns = pl.ds(pl.multiple_of((hi * NZ + zz) * OUT, OUT), OUT)
                weights.append(
                    push(
                        weight.at[pl.ds(half_rows, HEAD // 2), columns],
                        wbuf.at[pl.ds(d * HEAD + half_rows, HEAD // 2), pl.ds(part * OUT, OUT)],
                        at_z(d),
                    )
                )

    def ring_x(yx):
        along_x(yx, kslot(yx, 0), vslot(yx, 0))

    def take(*pairs):
        for yx, dx in pairs:
            landed(yx, dx, 0)
            across(yx, dx)

    def pass_on(yx):
        landed(yx, 3, 0)
        push_k(kslot(yx, 3), yx, 2, 0, at_x(1))
        landed(yx, 1, 0)
        push_v(vslot(yx, 1), yx, 2, 0, at_x(-1))
        across(yx, 3)
        across(yx, 1)

    both(0, 0)
    work(((0, 0),), (0,), True)
    ask = push(queries, qbuf.at[pl.ds(TOK, TOK)], at_y(toward))
    landed(1, 0, 0)
    ring_x(1)
    across(1, 0)
    take((3, 0))
    push_k(tokens(keys, y + 2), 2, 0, 0, at_y(2))
    push_v(tokens(values, y - 2), 2, 0, 0, at_y(-2))
    both(1, 0)
    both(3, 0)
    work(((1, 0), (3, 0)), (0,))
    ring_x(3)
    ask.wait_recv()
    work(((0, 0), (1, 0), (3, 0)), (1,), True)
    send_weights()
    group = ((0, 1), (0, 3), (0, 2))
    take(*group)
    landed(2, 0, 0)
    ring_x(2)
    across(2, 0)
    for pair in group:
        both(*pair)
    work(group, (0, 1))
    pass_on(1)
    group = ((1, 1), (1, 3), (2, 0))
    for pair in group:
        both(*pair)
    work(group, (0, 1))
    pass_on(3)
    group = ((3, 1), (3, 3))
    for pair in group:
        both(*pair)
    work(group, (0, 1))
    pass_on(2)
    take((1, 2))
    group = ((2, 1), (2, 3), (1, 2))
    for pair in group:
        both(*pair)
    work(group, (0, 1))
    for copy in weights:
        copy.wait_recv()
    across_rows = [wbuf.at[pl.ds(d * HEAD + half_rows, HEAD // 2)] for d in range(1, NZ)]
    shared = [push(rows, rows, sibling) for rows in across_rows]
    take((3, 2), (2, 2))
    both(3, 2)
    both(2, 2)

    given = []
    lane = lax.broadcasted_iota(jnp.int32, (STAT, HEAD), 1)

    def hand_over(side, block):
        if side == 0:
            return
        for part in range(block * ROWS // STAT, (block + 1) * ROWS // STAT):
            at, rows = pl.ds(TOK + part * STAT, STAT), pl.ds(part * STAT, STAT)
            give[rows, :] = acc[at, :HEAD].astype(jnp.bfloat16)
            give_stat[part] = jnp.where(lane == 0, peak[at, :], acc[at, HEAD:]).T[:8, :]
            given.append(
                (
                    push(give.at[rows], got.at[rows], at_y(toward)),
                    push(give_stat.at[part], got_stat.at[part], at_y(toward)),
                )
            )

    work(((3, 2), (2, 2)), (1, 0), after=hand_over)

    rings = {}

    def rows_of(cut):
        return pl.ds(cut * CUT, CUT)

    def at_cut(cut, d):
        return around.at[rows_of(cut), pl.ds(d * HEAD, HEAD)]

    def send_z(cut, src, d, hop):
        rings[cut, d] = push(at_cut(cut, src), at_cut(cut, d), at_z(hop))

    def combine(part):
        rows = pl.ds(part * STAT, STAT)
        for copy in given[part]:
            copy.wait_recv()
        stat = jnp.concatenate([got_stat[part], jnp.zeros((STAT - 8, HEAD), jnp.float32)], axis=0).T
        peak_two, sum_two = stat[:, 0:1], stat[:, 1:2]
        peak_one, sum_one = peak[rows, :], acc[rows, HEAD:]
        top = jnp.maximum(peak_one, peak_two)
        one, two = jnp.exp2(peak_one - top), jnp.exp2(peak_two - top)
        total = acc[rows, :HEAD] * one + got[rows, :].astype(jnp.float32) * two
        around[rows, pl.ds(0, HEAD)] = (total / (sum_one * one + sum_two * two)).astype(jnp.bfloat16)

    def begin(cut):
        if cut * CUT % STAT == 0:
            combine(cut * CUT // STAT)
        send_z(cut, 0, 1, 1)
        send_z(cut, 0, NZ - 1, -1)
        if cut in DIRECT:
            send_z(cut, 0, 2, 2)
            send_z(cut, 0, NZ - 2, -2)

    def onward(cut, stage):
        if cut in DIRECT:
            if stage == 1:
                rings[cut, 2].wait_recv()
                send_z(cut, 2, 3, 1)
                if cut % 2 == 0:
                    send_z(cut, 2, 4, 2)
                rings[cut, NZ - 2].wait_recv()
                send_z(cut, NZ - 2, NZ - 3, -1)
                if cut % 2 == 1:
                    send_z(cut, NZ - 2, 4, -2)
            return
        rings[cut, stage].wait_recv()
        if stage < 3 or cut % 2 == 0:
            send_z(cut, stage, stage + 1, 1)
        rings[cut, NZ - stage].wait_recv()
        if stage < 3 or cut % 2 == 1:
            send_z(cut, NZ - stage, NZ - stage - 1, -1)

    swaps = []

    def project(cut):
        for d in (1, 7, 3, 5) if cut in DIRECT else ():
            rings[cut, d].wait_recv()
        rings[cut, 4].wait_recv()
        rows = rows_of(cut)
        part = jnp.dot(around[rows, :], wbuf[...], preferred_element_type=jnp.float32)
        own_part[rows, :] = part[:, :OUT]
        swap[rows, :] = part[:, OUT:].astype(jnp.bfloat16)
        swaps.append(push(swap.at[rows], swapped.at[rows], opposite))

    for copy in shared:
        copy.wait_recv()
    for cut, stage in TURNS:
        if stage == 0:
            begin(cut)
        elif stage == 4:
            project(cut)
        else:
            onward(cut, stage)
    for cut in range(CUTS):
        rows = rows_of(cut)
        swaps[cut].wait_recv()
        out[rows, :] = (own_part[rows, :] + swapped[rows, :].astype(jnp.float32)).astype(jnp.bfloat16)
    for copy in started:
        copy.wait_send()


def local(queries, keys, values, out_weight, slot_span):
    vmem, anywhere = pl.BlockSpec(memory_space=pltpu.VMEM), pl.BlockSpec(memory_space=pl.ANY)
    return pl.pallas_call(
        kernel,
        out_shape=jax.ShapeDtypeStruct((TOK, OUT), jnp.bfloat16),
        in_specs=[pl.BlockSpec(memory_space=pltpu.SMEM), vmem, vmem, vmem, anywhere],
        out_specs=vmem,
        scratch_shapes=[
            pltpu.VMEM((2 * TOK, HEAD), jnp.bfloat16),
            pltpu.VMEM((4, NX, 2, HALF, HEAD), jnp.bfloat16),
            pltpu.VMEM((4, NX, 2, HALF, 2 * HEAD), jnp.bfloat16),
            pltpu.VMEM((NZ * HEAD, 2 * OUT), jnp.bfloat16),
            pltpu.VMEM((2 * TOK, 2 * HEAD), jnp.float32),
            pltpu.VMEM((2 * TOK, HEAD), jnp.float32),
            pltpu.VMEM((TOK, NZ * HEAD), jnp.bfloat16),
            pltpu.VMEM((TOK, HEAD), jnp.bfloat16),
            pltpu.VMEM((TOK, HEAD), jnp.bfloat16),
            pltpu.VMEM((TOK // STAT, 8, STAT), jnp.float32),
            pltpu.VMEM((TOK // STAT, 8, STAT), jnp.float32),
            pltpu.VMEM((TOK, OUT), jnp.float32),
            pltpu.VMEM((TOK, OUT), jnp.bfloat16),
            pltpu.VMEM((TOK, OUT), jnp.bfloat16),
            pltpu.SemaphoreType.DMA((COPIES,)),
            pltpu.SemaphoreType.DMA((COPIES,)),
            pltpu.SemaphoreType.DMA((5,)),
        ],
        compiler_params=pltpu.CompilerParams(
            collective_id=0, has_side_effects=True, vmem_limit_bytes=56 * 2**20
        ),
        cost_estimate=pl.CostEstimate(flops=9 * 10**9, bytes_accessed=3 * 10**6, transcendentals=9 * 10**6),
        name="attend_and_project",
    )(slot_span, queries, keys, values, out_weight)


def solution(mesh):
    in_specs = (P("row", "col"), P("row", None), P("row", None), P("col", None), P())
    return jax.shard_map(local, mesh=mesh, in_specs=in_specs, out_specs=P("row", "col"), check_vma=False)
```

```python
import math

import jax
import jax.numpy as jnp
from jax import lax
from jax.experimental import pallas as pl
from jax.experimental.pallas import tpu as pltpu
from jax.sharding import PartitionSpec as P

MESH = pl.DeviceIdType.MESH
TOK = 512
HALF = TOK // 2
HEAD = 128
NX, NY, NZ = 4, 8, 8
OUT = 256
ROWS = 256
STAT = 128
NB = TOK // ROWS
FLOOR = -1e30
HIDDEN = 3e30
SCALE = HEAD**-0.5 * math.log2(math.e)

COPIES = 180
CUTS = 4
CUT = TOK // CUTS
LAG = 1
DIRECT = ()
TURNS = [(cut, stage) for stage in range(5) for cut in range(CUTS)]


def kernel(
    span, queries_in, keys_in, values_in, weight_in, out,
    queries, keys, values, weight, qbuf, kbuf, vbuf, wbuf, acc, peak, around, give, got, give_stat, got_stat, own_part, swap, swapped,
    send_sem, recv_sem, local_sem,
):
    row, col = lax.axis_index("row"), lax.axis_index("col")
    core, x, ylo = row % 2, (row // 2) % NX, row // (2 * NX)
    z, yhi = col % NZ, col // NZ
    y = yhi * 4 + ylo
    parity = y % 2
    toward = 1 - 2 * parity

    def device(xx, yy, zz, cc):
        xx, yy, zz = (xx + NX) % NX, (yy + NY) % NY, (zz + NZ) % NZ
        return (((yy % 4) * NX + xx) * 2 + cc, (yy // 4) * NZ + zz)

    def slot_row(yx, dx, dc):
        yy = (ylo // 2 + yx // 2) % 2 * 2 + (ylo + yx) % 2
        return (yy * NX + (x + dx) % NX) * 2 + (core + dc) % 2

    def at_y(dy):
        return device(x, y + dy, z, core)

    def at_x(dx):
        return device(x + dx, y, z, core)

    def at_z(dz):
        return device(x, y, z + dz, core)

    sibling = device(x, y, z, (core + 1) % 2)
    opposite = device(x, y + 4, z, core)

    barrier = pltpu.get_barrier_semaphore()
    peers = [at_y(toward), at_y(-toward), at_y(2), at_y(-2), opposite, at_x(1), at_x(-1), sibling]
    peers += [at_z(d) for d in range(1, NZ)]
    for peer in peers:
        pl.semaphore_signal(barrier, inc=1, device_id=peer, device_id_type=MESH)

    whole = [
        pltpu.make_async_copy(src, dst, local_sem.at[5 + n])
        for n, (src, dst) in enumerate(
            ((keys_in, keys), (values_in, values), (queries_in, queries), (weight_in, weight))
        )
    ]
    for copy in whole:
        copy.start()

    vbuf[:, :, :, :, HEAD:] = jnp.ones((4, NX, 2, HALF, HEAD), jnp.bfloat16)

    def tokens(ref, yy):
        yy = (yy + NY) % NY
        group = (yy // 4) * 2 + z // 4
        start = pl.multiple_of((yy % 2) * HALF, HALF)
        return ref.at[pl.ds(start, HALF), pl.ds(pl.multiple_of(group * HEAD, HEAD), HEAD)]

    def kslot(yx, dx, dc=0):
        return kbuf.at[yx, dx, dc]

    def vslot(yx, dx, dc=0):
        return vbuf.at[yx, dx, dc, :, pl.ds(0, HEAD)]

    own_weight = pl.ds(pl.multiple_of(col * OUT, OUT), OUT)
    other_weight = pl.ds(pl.multiple_of((1 - yhi) * (NZ * OUT) + z * OUT, OUT), OUT)
    here = [
        pltpu.make_async_copy(tokens(keys, y), kslot(0, 0), local_sem.at[0]),
        pltpu.make_async_copy(tokens(values, y), vslot(0, 0), local_sem.at[1]),
        pltpu.make_async_copy(queries, qbuf.at[pl.ds(0, TOK)], local_sem.at[2]),
        pltpu.make_async_copy(weight.at[:, own_weight], wbuf.at[pl.ds(0, HEAD), pl.ds(0, OUT)], local_sem.at[3]),
        pltpu.make_async_copy(weight.at[:, other_weight], wbuf.at[pl.ds(0, HEAD), pl.ds(OUT, OUT)], local_sem.at[4]),
    ]
    for copy in whole[:3]:
        copy.wait()
    for copy in here[:3]:
        copy.start()
    whole[3].wait()
    for copy in here[3:]:
        copy.start()
    pl.semaphore_wait(barrier, len(peers))

    started = []

    def push(src, dst, to):
        k = len(started)
        copy = pltpu.make_async_remote_copy(
            src_ref=src, dst_ref=dst, send_sem=send_sem.at[k], recv_sem=recv_sem.at[k], device_id=to, device_id_type=MESH
        )
        copy.start()
        started.append(copy)
        return copy

    arriving = {}

    def push_k(src, yx, dx, dc, to):
        arriving[yx, dx, dc, 0] = push(src, kslot(yx, dx, dc), to)

    def push_v(src, yx, dx, dc, to):
        arriving[yx, dx, dc, 1] = push(src, vslot(yx, dx, dc), to)

    def landed(yx, dx, dc):
        arriving[yx, dx, dc, 0].wait_recv()
        arriving[yx, dx, dc, 1].wait_recv()

    def across(yx, dx):
        push_k(kslot(yx, dx), yx, dx, 1, sibling)
        push_v(vslot(yx, dx), yx, dx, 1, sibling)

    def along_x(yx, k, v):
        push_k(k, yx, 3, 0, at_x(1))
        push_k(k, yx, 1, 0, at_x(-1))
        push_v(v, yx, 3, 0, at_x(1))
        push_v(v, yx, 1, 0, at_x(-1))

    def both(yx, dx):
        landed(yx, dx, 1)

    push_k(tokens(keys, y + toward), 1, 0, 0, at_y(toward))
    push_k(tokens(keys, y - toward), 3, 0, 0, at_y(-toward))
    push_k(tokens(keys, y), 0, 0, 1, sibling)
    push_k(tokens(keys, y), 0, 3, 0, at_x(1))
    push_k(tokens(keys, y), 0, 1, 0, at_x(-1))
    push_v(tokens(values, y + toward), 1, 0, 0, at_y(toward))
    push_v(tokens(values, y - toward), 3, 0, 0, at_y(-toward))
    push_v(tokens(values, y), 0, 0, 1, sibling)
    push_v(tokens(values, y), 0, 3, 0, at_x(1))
    push_v(tokens(values, y), 0, 1, 0, at_x(-1))
    for copy in here:
        copy.wait()

    half_rows = pl.multiple_of(core * (HEAD // 2), HEAD // 2)
    weights = []

    def send_weights():
        for d in range(1, NZ):
            zz = (z + d) % NZ
            for part, hi in ((0, yhi), (1, 1 - yhi)):
                columns = pl.ds(pl.multiple_of((hi * NZ + zz) * OUT, OUT), OUT)
                weights.append(
                    push(
                        weight.at[pl.ds(half_rows, HEAD // 2), columns],
                        wbuf.at[pl.ds(d * HEAD + half_rows, HEAD // 2), pl.ds(part * OUT, OUT)],
                        at_z(d),
                    )
                )

    send_weights()
    my_span = (span[row], span[slot_row(1, 0, 0)])

    def hide(side, yx, dx, dc):
        return jnp.where(span[slot_row(yx, dx, dc)] < my_span[side], 0.0, HIDDEN).astype(jnp.float32)

    def at_block(side, block):
        return pl.ds(side * TOK + block * ROWS, ROWS)

    def score(group, side, block):
        query = qbuf[at_block(side, block), :]
        return [
            lax.dot_general(
                query, kbuf[yx, dx].reshape(TOK, HEAD), (((1,), (1,)), ((), ())), preferred_element_type=jnp.float32
            )
            for yx, dx in group
        ]

    def soften(group, side, block, scores, first):
        at = at_block(side, block)
        parts, top = [], None
        for (yx, dx), whole in zip(group, scores):
            for dc in range(2):
                if first and dc == 0 and (yx, side) in ((0, 0), (1, 1)):
                    i = lax.broadcasted_iota(jnp.int32, (ROWS, HEAD), 0) + block * ROWS
                    j = lax.broadcasted_iota(jnp.int32, (ROWS, HEAD), 1) + parity * HALF
                    seen, hidden = i - j, None
                else:
                    seen, hidden = None, hide(side, yx, dx, dc)
                pair = []
                for c in range(2):
                    part = whole[:, dc * HALF + c * HEAD : dc * HALF + (c + 1) * HEAD]
                    if seen is not None:
                        part = jnp.where(seen >= c * HEAD, part, jnp.float32(-HIDDEN))
                    pair.append(part)
                part_top = jnp.maximum(*pair)
                if hidden is not None:
                    part_top = part_top - hidden
                top = part_top if top is None else jnp.maximum(top, part_top)
                parts.append((pair, hidden))
        new = jnp.broadcast_to(jnp.max(top, axis=1, keepdims=True) * SCALE, (ROWS, HEAD))
        keep = None
        if first:
            new = jnp.maximum(new, jnp.float32(FLOOR))
        else:
            old = peak[at, :]
            new = jnp.maximum(old, new)
            keep = jnp.exp2(old - new)
        peak[at, :] = new
        shares = []
        for pair, hidden in parts:
            base = new if hidden is None else new + hidden
            shares += [jnp.exp2(part * SCALE - base).astype(jnp.bfloat16) for part in pair]
        return keep, shares

    def gather_in(group, side, block, keep, shares):
        at = at_block(side, block)
        total = None
        for n, (yx, dx) in enumerate(group):
            share = jnp.concatenate(shares[4 * n : 4 * n + 4], axis=1)
            value = vbuf[yx, dx].reshape(TOK, 2 * HEAD)
            term = jnp.dot(share, value, preferred_element_type=jnp.float32)
            total = term if total is None else total + term
        if keep is None:
            acc[at, :] = total
        else:
            acc[at, :HEAD] = acc[at, :HEAD] * keep + total[:, :HEAD]
            acc[at, HEAD:] = acc[at, HEAD:] * keep + total[:, HEAD:]

    def work(group, sides, first=False, after=None):
        blocks = [(side, block) for side in sides for block in range(NB)]
        scores = score(group, *blocks[0])
        for n, (side, block) in enumerate(blocks):
            later = score(group, *blocks[n + 1]) if n + 1 < len(blocks) else None
            gather_in(group, side, block, *soften(group, side, block, scores, first))
            scores = later
            if after is not None:
                after(side, block)

    def ring_x(yx):
        along_x(yx, kslot(yx, 0), vslot(yx, 0))

    def take(*pairs):
        for yx, dx in pairs:
            landed(yx, dx, 0)
            across(yx, dx)

    def pass_on(yx):
        landed(yx, 3, 0)
        push_k(kslot(yx, 3), yx, 2, 0, at_x(1))
        landed(yx, 1, 0)
        push_v(vslot(yx, 1), yx, 2, 0, at_x(-1))
        across(yx, 3)
        across(yx, 1)

    def work_on(*group):
        for pair in group:
            both(*pair)
        work(group, (0, 1))

    both(0, 0)
    work(((0, 0),), (0,), True)
    ask = push(queries, qbuf.at[pl.ds(TOK, TOK)], at_y(toward))
    landed(1, 0, 0)
    ring_x(1)
    across(1, 0)
    take((3, 0))
    push_k(tokens(keys, y + 2), 2, 0, 0, at_y(2))
    push_v(tokens(values, y - 2), 2, 0, 0, at_y(-2))
    pass_on(0)
    both(1, 0)
    both(3, 0)
    work(((1, 0), (3, 0)), (0,))
    ring_x(3)
    ask.wait_recv()
    work(((0, 0), (1, 0), (3, 0)), (1,), True)
    landed(2, 0, 0)
    ring_x(2)
    across(2, 0)
    take((0, 2))
    push_k(kslot(0, 2), 2, 2, 0, at_y(2 - 4 * (ylo // 2)))
    push_v(vslot(0, 2), 2, 2, 0, at_y(2 - 4 * (ylo // 2)))
    work_on((0, 1), (0, 3), (2, 0))
    pass_on(1)
    work_on((1, 1), (1, 3), (0, 2))
    pass_on(3)
    take((2, 2))
    work_on((3, 1), (3, 3), (2, 2))
    take((2, 1), (2, 3), (1, 2))
    work_on((2, 1), (2, 3), (1, 2))
    for copy in weights:
        copy.wait_recv()
    across_rows = [wbuf.at[pl.ds(d * HEAD + half_rows, HEAD // 2)] for d in range(1, NZ)]
    shared = [push(rows, rows, sibling) for rows in across_rows]
    take((3, 2))
    both(3, 2)

    given = []
    lane = lax.broadcasted_iota(jnp.int32, (STAT, HEAD), 1)

    def hand_over(side, block):
        if side == 0:
            return
        for part in range(block * ROWS // STAT, (block + 1) * ROWS // STAT):
            at, rows = pl.ds(TOK + part * STAT, STAT), pl.ds(part * STAT, STAT)
            give[rows, :] = acc[at, :HEAD].astype(jnp.bfloat16)
            give_stat[part] = jnp.where(lane == 0, peak[at, :], acc[at, HEAD:]).T[:8, :]
            given.append(
                (
                    push(give.at[rows], got.at[rows], at_y(toward)),
                    push(give_stat.at[part], got_stat.at[part], at_y(toward)),
                )
            )

    work(((3, 2),), (1, 0), after=hand_over)

    rings = {}

    def rows_of(cut):
        return pl.ds(cut * CUT, CUT)

    def at_cut(cut, d):
        return around.at[rows_of(cut), pl.ds(d * HEAD, HEAD)]

    def send_z(cut, src, d, hop):
        rings[cut, d] = push(at_cut(cut, src), at_cut(cut, d), at_z(hop))

    def combine(part):
        rows = pl.ds(part * STAT, STAT)
        for copy in given[part]:
            copy.wait_recv()
        stat = jnp.concatenate([got_stat[part], jnp.zeros((STAT - 8, HEAD), jnp.float32)], axis=0).T
        peak_two, sum_two = stat[:, 0:1], stat[:, 1:2]
        peak_one, sum_one = peak[rows, :], acc[rows, HEAD:]
        top = jnp.maximum(peak_one, peak_two)
        one, two = jnp.exp2(peak_one - top), jnp.exp2(peak_two - top)
        total = acc[rows, :HEAD] * one + got[rows, :].astype(jnp.float32) * two
        around[rows, pl.ds(0, HEAD)] = (total / (sum_one * one + sum_two * two)).astype(jnp.bfloat16)

    def begin(cut):
        if cut * CUT % STAT == 0:
            combine(cut * CUT // STAT)
        send_z(cut, 0, 1, 1)
        send_z(cut, 0, NZ - 1, -1)
        if cut in DIRECT:
            send_z(cut, 0, 2, 2)
            send_z(cut, 0, NZ - 2, -2)

    def onward(cut, stage):
        if cut in DIRECT:
            if stage == 1:
                rings[cut, 2].wait_recv()
                send_z(cut, 2, 3, 1)
                if cut % 2 == 0:
                    send_z(cut, 2, 4, 2)
                rings[cut, NZ - 2].wait_recv()
                send_z(cut, NZ - 2, NZ - 3, -1)
                if cut % 2 == 1:
                    send_z(cut, NZ - 2, 4, -2)
            return
        rings[cut, stage].wait_recv()
        if stage < 3 or cut % 2 == 0:
            send_z(cut, stage, stage + 1, 1)
        rings[cut, NZ - stage].wait_recv()
        if stage < 3 or cut % 2 == 1:
            send_z(cut, NZ - stage, NZ - stage - 1, -1)

    swaps = []

    def project(cut):
        for d in (1, 7, 3, 5) if cut in DIRECT else ():
            rings[cut, d].wait_recv()
        rings[cut, 4].wait_recv()
        rows = rows_of(cut)
        part = jnp.dot(around[rows, :], wbuf[...], preferred_element_type=jnp.float32)
        own_part[rows, :] = part[:, :OUT]
        swap[rows, :] = part[:, OUT:].astype(jnp.bfloat16)
        swaps.append(push(swap.at[rows], swapped.at[rows], opposite))

    for copy in shared:
        copy.wait_recv()
    for cut, stage in TURNS:
        if stage == 0:
            begin(cut)
        elif stage == 4:
            project(cut)
        else:
            onward(cut, stage)
    for cut in range(CUTS):
        rows = rows_of(cut)
        swaps[cut].wait_recv()
        out[rows, :] = (own_part[rows, :] + swapped[rows, :].astype(jnp.float32)).astype(jnp.bfloat16)
    for copy in started:
        copy.wait_send()


def local(queries, keys, values, out_weight, slot_span):
    vmem, anywhere = pl.BlockSpec(memory_space=pltpu.VMEM), pl.BlockSpec(memory_space=pl.ANY)
    return pl.pallas_call(
        kernel,
        out_shape=jax.ShapeDtypeStruct((TOK, OUT), jnp.bfloat16),
        in_specs=[pl.BlockSpec(memory_space=pltpu.SMEM)] + [anywhere] * 4,
        out_specs=vmem,
        scratch_shapes=[
            pltpu.VMEM((TOK, HEAD), jnp.bfloat16),
            pltpu.VMEM((TOK, 4 * HEAD), jnp.bfloat16),
            pltpu.VMEM((TOK, 4 * HEAD), jnp.bfloat16),
            pltpu.VMEM((HEAD, 2 * NZ * OUT), jnp.bfloat16),
            pltpu.VMEM((2 * TOK, HEAD), jnp.bfloat16),
            pltpu.VMEM((4, NX, 2, HALF, HEAD), jnp.bfloat16),
            pltpu.VMEM((4, NX, 2, HALF, 2 * HEAD), jnp.bfloat16),
            pltpu.VMEM((NZ * HEAD, 2 * OUT), jnp.bfloat16),
            pltpu.VMEM((2 * TOK, 2 * HEAD), jnp.float32),
            pltpu.VMEM((2 * TOK, HEAD), jnp.float32),
            pltpu.VMEM((TOK, NZ * HEAD), jnp.bfloat16),
            pltpu.VMEM((TOK, HEAD), jnp.bfloat16),
            pltpu.VMEM((TOK, HEAD), jnp.bfloat16),
            pltpu.VMEM((TOK // STAT, 8, STAT), jnp.float32),
            pltpu.VMEM((TOK // STAT, 8, STAT), jnp.float32),
            pltpu.VMEM((TOK, OUT), jnp.float32),
            pltpu.VMEM((TOK, OUT), jnp.bfloat16),
            pltpu.VMEM((TOK, OUT), jnp.bfloat16),
            pltpu.SemaphoreType.DMA((COPIES,)),
            pltpu.SemaphoreType.DMA((COPIES,)),
            pltpu.SemaphoreType.DMA((9,)),
        ],
        compiler_params=pltpu.CompilerParams(
            collective_id=0, has_side_effects=True, vmem_limit_bytes=56 * 2**20
        ),
        cost_estimate=pl.CostEstimate(flops=9 * 10**9, bytes_accessed=3 * 10**6, transcendentals=9 * 10**6),
        name="attend_and_project",
    )(slot_span, queries, keys, values, out_weight)


def solution(mesh):
    in_specs = (P("row", "col"), P("row", None), P("row", None), P("col", None), P())
    return jax.shard_map(local, mesh=mesh, in_specs=in_specs, out_specs=P("row", "col"), check_vma=False)
```

```python
import math

import jax
import jax.numpy as jnp
from jax import lax
from jax.experimental import pallas as pl
from jax.experimental.pallas import tpu as pltpu
from jax.sharding import PartitionSpec as P

MESH = pl.DeviceIdType.MESH
TOK = 512
HALF = TOK // 2
HEAD = 128
NX, NY, NZ = 4, 8, 8
OUT = 256
ROWS = 256
STAT = 128
NB = TOK // ROWS
FLOOR = -1e30
HIDDEN = 3e30
SCALE = HEAD**-0.5 * math.log2(math.e)

COPIES = 180
CUTS = 4
CUT = TOK // CUTS
LAG = 1
DIRECT = ()
TURNS = [(cut, stage) for stage in range(5) for cut in range(CUTS)]


def kernel(
    span, queries_in, keys_in, values_in, weight_in, out,
    queries, keys, values, weight, qbuf, kbuf, vbuf, wbuf, acc, peak, around, give, got, give_stat, got_stat, own_part, swap, swapped,
    send_sem, recv_sem, local_sem,
):
    row, col = lax.axis_index("row"), lax.axis_index("col")
    core, x, ylo = row % 2, (row // 2) % NX, row // (2 * NX)
    z, yhi = col % NZ, col // NZ
    y = yhi * 4 + ylo
    parity = y % 2
    toward = 1 - 2 * parity

    def device(xx, yy, zz, cc):
        xx, yy, zz = (xx + NX) % NX, (yy + NY) % NY, (zz + NZ) % NZ
        return (((yy % 4) * NX + xx) * 2 + cc, (yy // 4) * NZ + zz)

    def slot_row(yx, dx, dc):
        yy = (ylo // 2 + yx // 2) % 2 * 2 + (ylo + yx) % 2
        return (yy * NX + (x + dx) % NX) * 2 + (core + dc) % 2

    def at_y(dy):
        return device(x, y + dy, z, core)

    def at_x(dx):
        return device(x + dx, y, z, core)

    def at_z(dz):
        return device(x, y, z + dz, core)

    sibling = device(x, y, z, (core + 1) % 2)
    opposite = device(x, y + 4, z, core)

    barrier = pltpu.get_barrier_semaphore()
    peers = [at_y(toward), at_y(-toward), at_y(2), at_y(-2), opposite, at_x(1), at_x(-1), sibling]
    peers += [at_z(d) for d in range(1, NZ)]
    for peer in peers:
        pl.semaphore_signal(barrier, inc=1, device_id=peer, device_id_type=MESH)

    whole = [
        pltpu.make_async_copy(src, dst, local_sem.at[5 + n])
        for n, (src, dst) in enumerate(
            ((keys_in, keys), (values_in, values), (queries_in, queries), (weight_in, weight))
        )
    ]
    for copy in whole:
        copy.start()

    vbuf[:, :, :, :, HEAD:] = jnp.ones((4, NX, 2, HALF, HEAD), jnp.bfloat16)

    def tokens(ref, yy):
        yy = (yy + NY) % NY
        group = (yy // 4) * 2 + z // 4
        start = pl.multiple_of((yy % 2) * HALF, HALF)
        return ref.at[pl.ds(start, HALF), pl.ds(pl.multiple_of(group * HEAD, HEAD), HEAD)]

    def kslot(yx, dx, dc=0):
        return kbuf.at[yx, dx, dc]

    def vslot(yx, dx, dc=0):
        return vbuf.at[yx, dx, dc, :, pl.ds(0, HEAD)]

    own_weight = pl.ds(pl.multiple_of(col * OUT, OUT), OUT)
    other_weight = pl.ds(pl.multiple_of((1 - yhi) * (NZ * OUT) + z * OUT, OUT), OUT)
    here = [
        pltpu.make_async_copy(tokens(keys, y), kslot(0, 0), local_sem.at[0]),
        pltpu.make_async_copy(tokens(values, y), vslot(0, 0), local_sem.at[1]),
        pltpu.make_async_copy(queries, qbuf.at[pl.ds(0, TOK)], local_sem.at[2]),
        pltpu.make_async_copy(weight.at[:, own_weight], wbuf.at[pl.ds(0, HEAD), pl.ds(0, OUT)], local_sem.at[3]),
        pltpu.make_async_copy(weight.at[:, other_weight], wbuf.at[pl.ds(0, HEAD), pl.ds(OUT, OUT)], local_sem.at[4]),
    ]
    for copy in whole[:3]:
        copy.wait()
    for copy in here[:3]:
        copy.start()
    whole[3].wait()
    for copy in here[3:]:
        copy.start()
    pl.semaphore_wait(barrier, len(peers))

    started = []

    def push(src, dst, to):
        k = len(started)
        copy = pltpu.make_async_remote_copy(
            src_ref=src, dst_ref=dst, send_sem=send_sem.at[k], recv_sem=recv_sem.at[k], device_id=to, device_id_type=MESH
        )
        copy.start()
        started.append(copy)
        return copy

    arriving = {}

    def push_k(src, yx, dx, dc, to):
        arriving[yx, dx, dc, 0] = push(src, kslot(yx, dx, dc), to)

    def push_v(src, yx, dx, dc, to):
        arriving[yx, dx, dc, 1] = push(src, vslot(yx, dx, dc), to)

    def landed(yx, dx, dc):
        arriving[yx, dx, dc, 0].wait_recv()
        arriving[yx, dx, dc, 1].wait_recv()

    def across(yx, dx):
        push_k(kslot(yx, dx), yx, dx, 1, sibling)
        push_v(vslot(yx, dx), yx, dx, 1, sibling)

    def along_x(yx, k, v):
        push_k(k, yx, 3, 0, at_x(1))
        push_k(k, yx, 1, 0, at_x(-1))
        push_v(v, yx, 3, 0, at_x(1))
        push_v(v, yx, 1, 0, at_x(-1))

    def both(yx, dx):
        landed(yx, dx, 1)

    push_k(tokens(keys, y + toward), 1, 0, 0, at_y(toward))
    push_k(tokens(keys, y - toward), 3, 0, 0, at_y(-toward))
    push_k(tokens(keys, y), 0, 0, 1, sibling)
    push_k(tokens(keys, y), 0, 3, 0, at_x(1))
    push_k(tokens(keys, y), 0, 1, 0, at_x(-1))
    push_v(tokens(values, y + toward), 1, 0, 0, at_y(toward))
    push_v(tokens(values, y - toward), 3, 0, 0, at_y(-toward))
    push_v(tokens(values, y), 0, 0, 1, sibling)
    push_v(tokens(values, y), 0, 3, 0, at_x(1))
    push_v(tokens(values, y), 0, 1, 0, at_x(-1))
    for copy in here:
        copy.wait()

    half_rows = pl.multiple_of(core * (HEAD // 2), HEAD // 2)
    weights = []

    def send_weights():
        for d in range(1, NZ):
            zz = (z + d) % NZ
            for part, hi in ((0, yhi), (1, 1 - yhi)):
                columns = pl.ds(pl.multiple_of((hi * NZ + zz) * OUT, OUT), OUT)
                weights.append(
                    push(
                        weight.at[pl.ds(half_rows, HEAD // 2), columns],
                        wbuf.at[pl.ds(d * HEAD + half_rows, HEAD // 2), pl.ds(part * OUT, OUT)],
                        at_z(d),
                    )
                )

    send_weights()
    my_span = (span[row], span[slot_row(1, 0, 0)])

    def hide(side, yx, dx, dc):
        return jnp.where(span[slot_row(yx, dx, dc)] < my_span[side], 0.0, HIDDEN).astype(jnp.float32)

    def at_block(side, block):
        return pl.ds(side * TOK + block * ROWS, ROWS)

    def score(group, side, block):
        query = qbuf[at_block(side, block), :]
        return [
            lax.dot_general(
                query, kbuf[yx, dx].reshape(TOK, HEAD), (((1,), (1,)), ((), ())), preferred_element_type=jnp.float32
            )
            for yx, dx in group
        ]

    def soften(group, side, block, scores, first):
        at = at_block(side, block)
        parts, top = [], None
        for (yx, dx), whole in zip(group, scores):
            for dc in range(2):
                if first and dc == 0 and (yx, side) in ((0, 0), (1, 1)):
                    i = lax.broadcasted_iota(jnp.int32, (ROWS, HEAD), 0) + block * ROWS
                    j = lax.broadcasted_iota(jnp.int32, (ROWS, HEAD), 1) + parity * HALF
                    seen, hidden = i - j, None
                else:
                    seen, hidden = None, hide(side, yx, dx, dc)
                pair = []
                for c in range(2):
                    part = whole[:, dc * HALF + c * HEAD : dc * HALF + (c + 1) * HEAD]
                    if seen is not None:
                        part = jnp.where(seen >= c * HEAD, part, jnp.float32(-HIDDEN))
                    pair.append(part)
                part_top = jnp.maximum(*pair)
                if hidden is not None:
                    part_top = part_top - hidden
                top = part_top if top is None else jnp.maximum(top, part_top)
                parts.append((pair, hidden))
        new = jnp.broadcast_to(jnp.max(top, axis=1, keepdims=True) * SCALE, (ROWS, HEAD))
        keep = None
        if first:
            new = jnp.maximum(new, jnp.float32(FLOOR))
        else:
            old = peak[at, :]
            new = jnp.maximum(old, new)
            keep = jnp.exp2(old - new)
        peak[at, :] = new
        shares = []
        for pair, hidden in parts:
            base = new if hidden is None else new + hidden
            shares += [jnp.exp2(part * SCALE - base).astype(jnp.bfloat16) for part in pair]
        return keep, shares

    def gather_in(group, side, block, keep, shares):
        at = at_block(side, block)
        total = None
        for n, (yx, dx) in enumerate(group):
            share = jnp.concatenate(shares[4 * n : 4 * n + 4], axis=1)
            value = vbuf[yx, dx].reshape(TOK, 2 * HEAD)
            term = jnp.dot(share, value, preferred_element_type=jnp.float32)
            total = term if total is None else total + term
        if keep is None:
            acc[at, :] = total
        else:
            acc[at, :HEAD] = acc[at, :HEAD] * keep + total[:, :HEAD]
            acc[at, HEAD:] = acc[at, HEAD:] * keep + total[:, HEAD:]

    def work(group, sides, first=False, after=None):
        blocks = [(side, block) for side in sides for block in range(NB)]
        scores = score(group, *blocks[0])
        for n, (side, block) in enumerate(blocks):
            later = score(group, *blocks[n + 1]) if n + 1 < len(blocks) else None
            gather_in(group, side, block, *soften(group, side, block, scores, first))
            scores = later
            if after is not None:
                after(side, block)

    def ring_x(yx):
        along_x(yx, kslot(yx, 0), vslot(yx, 0))

    def take(*pairs):
        for yx, dx in pairs:
            landed(yx, dx, 0)
            across(yx, dx)

    def pass_on(yx):
        landed(yx, 3, 0)
        push_k(kslot(yx, 3), yx, 2, 0, at_x(1))
        landed(yx, 1, 0)
        push_v(vslot(yx, 1), yx, 2, 0, at_x(-1))
        across(yx, 3)
        across(yx, 1)

    def ready(*group):
        for pair in group:
            both(*pair)

    def work_on(*group, between=None):
        ready(*group)
        work(group, (0, 1), after=lambda side, block: between() if (side, block) == (0, NB - 1) and between else None)

    ready((0, 0))
    work(((0, 0),), (0,), True)
    ask = push(queries, qbuf.at[pl.ds(TOK, TOK)], at_y(toward))
    landed(1, 0, 0)
    ring_x(1)
    across(1, 0)
    take((3, 0))
    push_k(tokens(keys, y + 2), 2, 0, 0, at_y(2))
    push_v(tokens(values, y - 2), 2, 0, 0, at_y(-2))
    pass_on(0)
    ready((1, 0), (3, 0))
    work(((1, 0), (3, 0)), (0,))
    ring_x(3)
    ask.wait_recv()
    work(((0, 0), (1, 0), (3, 0)), (1,), True)
    landed(2, 0, 0)
    ring_x(2)
    across(2, 0)

    def far_on():
        take((0, 2))
        push_k(kslot(0, 2), 2, 2, 0, at_y(2 - 4 * (ylo // 2)))
        push_v(vslot(0, 2), 2, 2, 0, at_y(2 - 4 * (ylo // 2)))

    work_on((0, 1), (0, 3), between=far_on)
    pass_on(1)
    work_on((2, 0), (0, 2))
    work_on((1, 1), (1, 3), between=lambda: pass_on(3))
    take((2, 2))
    work_on((3, 1), (3, 3), between=lambda: take((2, 1), (2, 3)))
    take((1, 2))
    group, last = ((2, 1), (2, 3), (2, 2)), ((1, 2), (3, 2))
    ready(*group)
    work(group, (1,))
    take((3, 2))
    for copy in weights:
        copy.wait_recv()
    across_rows = [wbuf.at[pl.ds(d * HEAD + half_rows, HEAD // 2)] for d in range(1, NZ)]
    shared = [push(rows, rows, sibling) for rows in across_rows]
    ready(*last)

    given = []
    lane = lax.broadcasted_iota(jnp.int32, (STAT, HEAD), 1)

    def hand_over(side, block):
        if side == 0:
            return
        for part in range(block * ROWS // STAT, (block + 1) * ROWS // STAT):
            at, rows = pl.ds(TOK + part * STAT, STAT), pl.ds(part * STAT, STAT)
            give[rows, :] = acc[at, :HEAD].astype(jnp.bfloat16)
            give_stat[part] = jnp.where(lane == 0, peak[at, :], acc[at, HEAD:]).T[:8, :]
            given.append(
                (
                    push(give.at[rows], got.at[rows], at_y(toward)),
                    push(give_stat.at[part], got_stat.at[part], at_y(toward)),
                )
            )

    work(last, (1,), after=hand_over)
    work(group + last, (0,))

    rings = {}

    def rows_of(cut):
        return pl.ds(cut * CUT, CUT)

    def at_cut(cut, d):
        return around.at[rows_of(cut), pl.ds(d * HEAD, HEAD)]

    def send_z(cut, src, d, hop):
        rings[cut, d] = push(at_cut(cut, src), at_cut(cut, d), at_z(hop))

    def combine(part):
        rows = pl.ds(part * STAT, STAT)
        for copy in given[part]:
            copy.wait_recv()
        stat = jnp.concatenate([got_stat[part], jnp.zeros((STAT - 8, HEAD), jnp.float32)], axis=0).T
        peak_two, sum_two = stat[:, 0:1], stat[:, 1:2]
        peak_one, sum_one = peak[rows, :], acc[rows, HEAD:]
        top = jnp.maximum(peak_one, peak_two)
        one, two = jnp.exp2(peak_one - top), jnp.exp2(peak_two - top)
        total = acc[rows, :HEAD] * one + got[rows, :].astype(jnp.float32) * two
        around[rows, pl.ds(0, HEAD)] = (total / (sum_one * one + sum_two * two)).astype(jnp.bfloat16)

    def begin(cut):
        if cut * CUT % STAT == 0:
            combine(cut * CUT // STAT)
        send_z(cut, 0, 1, 1)
        send_z(cut, 0, NZ - 1, -1)
        if cut in DIRECT:
            send_z(cut, 0, 2, 2)
            send_z(cut, 0, NZ - 2, -2)

    def onward(cut, stage):
        if cut in DIRECT:
            if stage == 1:
                rings[cut, 2].wait_recv()
                send_z(cut, 2, 3, 1)
                if cut % 2 == 0:
                    send_z(cut, 2, 4, 2)
                rings[cut, NZ - 2].wait_recv()
                send_z(cut, NZ - 2, NZ - 3, -1)
                if cut % 2 == 1:
                    send_z(cut, NZ - 2, 4, -2)
            return
        rings[cut, stage].wait_recv()
        if stage < 3 or cut % 2 == 0:
            send_z(cut, stage, stage + 1, 1)
        rings[cut, NZ - stage].wait_recv()
        if stage < 3 or cut % 2 == 1:
            send_z(cut, NZ - stage, NZ - stage - 1, -1)

    swaps = []

    def project(cut):
        for d in (1, 7, 3, 5) if cut in DIRECT else ():
            rings[cut, d].wait_recv()
        rings[cut, 4].wait_recv()
        rows = rows_of(cut)
        part = jnp.dot(around[rows, :], wbuf[...], preferred_element_type=jnp.float32)
        own_part[rows, :] = part[:, :OUT]
        swap[rows, :] = part[:, OUT:].astype(jnp.bfloat16)
        swaps.append(push(swap.at[rows], swapped.at[rows], opposite))

    for copy in shared:
        copy.wait_recv()
    for cut, stage in TURNS:
        if stage == 0:
            begin(cut)
        elif stage == 4:
            project(cut)
        else:
            onward(cut, stage)
    for cut in range(CUTS):
        rows = rows_of(cut)
        swaps[cut].wait_recv()
        out[rows, :] = (own_part[rows, :] + swapped[rows, :].astype(jnp.float32)).astype(jnp.bfloat16)
    for copy in started:
        copy.wait_send()


def local(queries, keys, values, out_weight, slot_span):
    vmem, anywhere = pl.BlockSpec(memory_space=pltpu.VMEM), pl.BlockSpec(memory_space=pl.ANY)
    return pl.pallas_call(
        kernel,
        out_shape=jax.ShapeDtypeStruct((TOK, OUT), jnp.bfloat16),
        in_specs=[pl.BlockSpec(memory_space=pltpu.SMEM)] + [anywhere] * 4,
        out_specs=vmem,
        scratch_shapes=[
            pltpu.VMEM((TOK, HEAD), jnp.bfloat16),
            pltpu.VMEM((TOK, 4 * HEAD), jnp.bfloat16),
            pltpu.VMEM((TOK, 4 * HEAD), jnp.bfloat16),
            pltpu.VMEM((HEAD, 2 * NZ * OUT), jnp.bfloat16),
            pltpu.VMEM((2 * TOK, HEAD), jnp.bfloat16),
            pltpu.VMEM((4, NX, 2, HALF, HEAD), jnp.bfloat16),
            pltpu.VMEM((4, NX, 2, HALF, 2 * HEAD), jnp.bfloat16),
            pltpu.VMEM((NZ * HEAD, 2 * OUT), jnp.bfloat16),
            pltpu.VMEM((2 * TOK, 2 * HEAD), jnp.float32),
            pltpu.VMEM((2 * TOK, HEAD), jnp.float32),
            pltpu.VMEM((TOK, NZ * HEAD), jnp.bfloat16),
            pltpu.VMEM((TOK, HEAD), jnp.bfloat16),
            pltpu.VMEM((TOK, HEAD), jnp.bfloat16),
            pltpu.VMEM((TOK // STAT, 8, STAT), jnp.float32),
            pltpu.VMEM((TOK // STAT, 8, STAT), jnp.float32),
            pltpu.VMEM((TOK, OUT), jnp.float32),
            pltpu.VMEM((TOK, OUT), jnp.bfloat16),
            pltpu.VMEM((TOK, OUT), jnp.bfloat16),
            pltpu.SemaphoreType.DMA((COPIES,)),
            pltpu.SemaphoreType.DMA((COPIES,)),
            pltpu.SemaphoreType.DMA((9,)),
        ],
        compiler_params=pltpu.CompilerParams(
            collective_id=0, has_side_effects=True, vmem_limit_bytes=56 * 2**20
        ),
        cost_estimate=pl.CostEstimate(flops=9 * 10**9, bytes_accessed=3 * 10**6, transcendentals=9 * 10**6),
        name="attend_and_project",
    )(slot_span, queries, keys, values, out_weight)


def solution(mesh):
    in_specs = (P("row", "col"), P("row", None), P("row", None), P("col", None), P())
    return jax.shard_map(local, mesh=mesh, in_specs=in_specs, out_specs=P("row", "col"), check_vma=False)
```

```python
import math

import jax
import jax.numpy as jnp
from jax import lax
from jax.experimental import pallas as pl
from jax.experimental.pallas import tpu as pltpu
from jax.sharding import PartitionSpec as P

MESH = pl.DeviceIdType.MESH
TOK = 512
HALF = TOK // 2
HEAD = 128
NX, NY, NZ = 4, 8, 8
OUT = 256
ROWS = 256
STAT = 128
NB = TOK // ROWS
FLOOR = -1e30
HIDDEN = 3e30
SCALE = HEAD**-0.5 * math.log2(math.e)

COPIES = 180
CUTS = 4
CUT = TOK // CUTS
LAG = 1
DIRECT = ()
TURNS = [(0,0),(1,0),(2,0),(3,0),(0,1),(1,1),(2,1),(3,1),(0,2),(1,2),(2,2),(3,2),(0,3),(1,3),(0,4),(2,3),(1,4),(3,3),(2,4),(3,4)]


def kernel(
    span, queries_in, keys_in, values_in, weight_in, out,
    queries, keys, values, weight, qbuf, kbuf, vbuf, wbuf, acc, peak, around, give, got, give_stat, got_stat, own_part, swap, swapped,
    send_sem, recv_sem, local_sem,
):
    row, col = lax.axis_index("row"), lax.axis_index("col")
    core, x, ylo = row % 2, (row // 2) % NX, row // (2 * NX)
    z, yhi = col % NZ, col // NZ
    y = yhi * 4 + ylo
    parity = y % 2
    toward = 1 - 2 * parity

    def device(xx, yy, zz, cc):
        xx, yy, zz = (xx + NX) % NX, (yy + NY) % NY, (zz + NZ) % NZ
        return (((yy % 4) * NX + xx) * 2 + cc, (yy // 4) * NZ + zz)

    def slot_row(yx, dx, dc):
        yy = (ylo // 2 + yx // 2) % 2 * 2 + (ylo + yx) % 2
        return (yy * NX + (x + dx) % NX) * 2 + (core + dc) % 2

    def at_y(dy):
        return device(x, y + dy, z, core)

    def at_x(dx):
        return device(x + dx, y, z, core)

    def at_z(dz):
        return device(x, y, z + dz, core)

    sibling = device(x, y, z, (core + 1) % 2)
    opposite = device(x, y + 4, z, core)

    barrier = pltpu.get_barrier_semaphore()
    peers = [at_y(toward), at_y(-toward), at_y(2), at_y(-2), opposite, at_x(1), at_x(-1), sibling]
    peers += [at_z(d) for d in range(1, NZ)]
    for peer in peers:
        pl.semaphore_signal(barrier, inc=1, device_id=peer, device_id_type=MESH)

    whole = [
        pltpu.make_async_copy(src, dst, local_sem.at[5 + n])
        for n, (src, dst) in enumerate(
            ((keys_in, keys), (values_in, values), (queries_in, queries), (weight_in, weight))
        )
    ]
    for copy in whole:
        copy.start()

    vbuf[:, :, :, :, HEAD:] = jnp.ones((4, NX, 2, HALF, HEAD), jnp.bfloat16)

    def tokens(ref, yy):
        yy = (yy + NY) % NY
        group = (yy // 4) * 2 + z // 4
        start = pl.multiple_of((yy % 2) * HALF, HALF)
        return ref.at[pl.ds(start, HALF), pl.ds(pl.multiple_of(group * HEAD, HEAD), HEAD)]

    def kslot(yx, dx, dc=0):
        return kbuf.at[yx, dx, dc]

    def vslot(yx, dx, dc=0):
        return vbuf.at[yx, dx, dc, :, pl.ds(0, HEAD)]

    own_weight = pl.ds(pl.multiple_of(col * OUT, OUT), OUT)
    other_weight = pl.ds(pl.multiple_of((1 - yhi) * (NZ * OUT) + z * OUT, OUT), OUT)
    here = [
        pltpu.make_async_copy(tokens(keys, y), kslot(0, 0), local_sem.at[0]),
        pltpu.make_async_copy(tokens(values, y), vslot(0, 0), local_sem.at[1]),
        pltpu.make_async_copy(queries, qbuf.at[pl.ds(0, TOK)], local_sem.at[2]),
        pltpu.make_async_copy(weight.at[:, own_weight], wbuf.at[pl.ds(0, HEAD), pl.ds(0, OUT)], local_sem.at[3]),
        pltpu.make_async_copy(weight.at[:, other_weight], wbuf.at[pl.ds(0, HEAD), pl.ds(OUT, OUT)], local_sem.at[4]),
    ]
    for copy in whole[:3]:
        copy.wait()
    for copy in here[:3]:
        copy.start()
    whole[3].wait()
    for copy in here[3:]:
        copy.start()
    pl.semaphore_wait(barrier, len(peers))

    started = []

    def push(src, dst, to):
        k = len(started)
        copy = pltpu.make_async_remote_copy(
            src_ref=src, dst_ref=dst, send_sem=send_sem.at[k], recv_sem=recv_sem.at[k], device_id=to, device_id_type=MESH
        )
        copy.start()
        started.append(copy)
        return copy

    arriving = {}

    def push_k(src, yx, dx, dc, to):
        arriving[yx, dx, dc, 0] = push(src, kslot(yx, dx, dc), to)

    def push_v(src, yx, dx, dc, to):
        arriving[yx, dx, dc, 1] = push(src, vslot(yx, dx, dc), to)

    def landed(yx, dx, dc):
        arriving[yx, dx, dc, 0].wait_recv()
        arriving[yx, dx, dc, 1].wait_recv()

    def across(yx, dx):
        push_k(kslot(yx, dx), yx, dx, 1, sibling)
        push_v(vslot(yx, dx), yx, dx, 1, sibling)

    def along_x(yx, k, v):
        push_k(k, yx, 3, 0, at_x(1))
        push_k(k, yx, 1, 0, at_x(-1))
        push_v(v, yx, 3, 0, at_x(1))
        push_v(v, yx, 1, 0, at_x(-1))

    def both(yx, dx):
        landed(yx, dx, 1)

    push_k(tokens(keys, y + toward), 1, 0, 0, at_y(toward))
    push_k(tokens(keys, y - toward), 3, 0, 0, at_y(-toward))
    push_k(tokens(keys, y), 0, 0, 1, sibling)
    push_k(tokens(keys, y), 0, 3, 0, at_x(1))
    push_k(tokens(keys, y), 0, 1, 0, at_x(-1))
    push_v(tokens(values, y + toward), 1, 0, 0, at_y(toward))
    push_v(tokens(values, y - toward), 3, 0, 0, at_y(-toward))
    push_v(tokens(values, y), 0, 0, 1, sibling)
    push_v(tokens(values, y), 0, 3, 0, at_x(1))
    push_v(tokens(values, y), 0, 1, 0, at_x(-1))
    for copy in here:
        copy.wait()

    half_rows = pl.multiple_of(core * (HEAD // 2), HEAD // 2)
    weights = []

    def send_weights():
        for d in range(1, NZ):
            zz = (z + d) % NZ
            for part, hi in ((0, yhi), (1, 1 - yhi)):
                columns = pl.ds(pl.multiple_of((hi * NZ + zz) * OUT, OUT), OUT)
                weights.append(
                    push(
                        weight.at[pl.ds(half_rows, HEAD // 2), columns],
                        wbuf.at[pl.ds(d * HEAD + half_rows, HEAD // 2), pl.ds(part * OUT, OUT)],
                        at_z(d),
                    )
                )

    send_weights()
    my_span = (span[row], span[slot_row(1, 0, 0)])

    def hide(side, yx, dx, dc):
        return jnp.where(span[slot_row(yx, dx, dc)] < my_span[side], 0.0, HIDDEN).astype(jnp.float32)

    def at_block(side, block):
        return pl.ds(side * TOK + block * ROWS, ROWS)

    def score(group, side, block):
        query = qbuf[at_block(side, block), :]
        return [
            lax.dot_general(
                query, kbuf[yx, dx].reshape(TOK, HEAD), (((1,), (1,)), ((), ())), preferred_element_type=jnp.float32
            )
            for yx, dx in group
        ]

    def soften(group, side, block, scores, first):
        at = at_block(side, block)
        parts, top = [], None
        for (yx, dx), whole in zip(group, scores):
            for dc in range(2):
                if first and dc == 0 and (yx, side) in ((0, 0), (1, 1)):
                    i = lax.broadcasted_iota(jnp.int32, (ROWS, HEAD), 0) + block * ROWS
                    j = lax.broadcasted_iota(jnp.int32, (ROWS, HEAD), 1) + parity * HALF
                    seen, hidden = i - j, None
                else:
                    seen, hidden = None, hide(side, yx, dx, dc)
                pair = []
                for c in range(2):
                    part = whole[:, dc * HALF + c * HEAD : dc * HALF + (c + 1) * HEAD]
                    if seen is not None:
                        part = jnp.where(seen >= c * HEAD, part, jnp.float32(-HIDDEN))
                    pair.append(part)
                part_top = jnp.maximum(*pair)
                if hidden is not None:
                    part_top = part_top - hidden
                top = part_top if top is None else jnp.maximum(top, part_top)
                parts.append((pair, hidden))
        new = jnp.broadcast_to(jnp.max(top, axis=1, keepdims=True) * SCALE, (ROWS, HEAD))
        keep = None
        if first:
            new = jnp.maximum(new, jnp.float32(FLOOR))
        else:
            old = peak[at, :]
            new = jnp.maximum(old, new)
            keep = jnp.exp2(old - new)
        peak[at, :] = new
        shares = []
        for pair, hidden in parts:
            base = new if hidden is None else new + hidden
            shares += [jnp.exp2(part * SCALE - base).astype(jnp.bfloat16) for part in pair]
        return keep, shares

    def gather_in(group, side, block, keep, shares):
        at = at_block(side, block)
        total = None
        for n, (yx, dx) in enumerate(group):
            share = jnp.concatenate(shares[4 * n : 4 * n + 4], axis=1)
            value = vbuf[yx, dx].reshape(TOK, 2 * HEAD)
            term = jnp.dot(share, value, preferred_element_type=jnp.float32)
            total = term if total is None else total + term
        if keep is None:
            acc[at, :] = total
        else:
            acc[at, :HEAD] = acc[at, :HEAD] * keep + total[:, :HEAD]
            acc[at, HEAD:] = acc[at, HEAD:] * keep + total[:, HEAD:]

    def work(group, sides, first=False, after=None):
        blocks = [(side, block) for side in sides for block in range(NB)]
        scores = score(group, *blocks[0])
        for n, (side, block) in enumerate(blocks):
            later = score(group, *blocks[n + 1]) if n + 1 < len(blocks) else None
            gather_in(group, side, block, *soften(group, side, block, scores, first))
            scores = later
            if after is not None:
                after(side, block)

    def ring_x(yx):
        along_x(yx, kslot(yx, 0), vslot(yx, 0))

    def take(*pairs):
        for yx, dx in pairs:
            landed(yx, dx, 0)
            across(yx, dx)

    def pass_on(yx):
        landed(yx, 3, 0)
        push_k(kslot(yx, 3), yx, 2, 0, at_x(1))
        landed(yx, 1, 0)
        push_v(vslot(yx, 1), yx, 2, 0, at_x(-1))
        across(yx, 3)
        across(yx, 1)

    def ready(*group):
        for pair in group:
            both(*pair)

    def work_on(*group, between=None):
        ready(*group)
        work(group, (0, 1), after=lambda side, block: between() if (side, block) == (0, NB - 1) and between else None)

    ready((0, 0))
    work(((0, 0),), (0,), True)
    ask = push(queries, qbuf.at[pl.ds(TOK, TOK)], at_y(toward))
    landed(1, 0, 0)
    ring_x(1)
    across(1, 0)
    take((3, 0))
    push_k(tokens(keys, y + 2), 2, 0, 0, at_y(2))
    push_v(tokens(values, y - 2), 2, 0, 0, at_y(-2))
    pass_on(0)
    ready((1, 0), (3, 0))
    work(((1, 0), (3, 0)), (0,))
    ring_x(3)
    ask.wait_recv()
    work(((0, 0), (1, 0), (3, 0)), (1,), True)
    landed(2, 0, 0)
    ring_x(2)
    across(2, 0)

    def far_on():
        take((0, 2))
        push_k(kslot(0, 2), 2, 2, 0, at_y(2 - 4 * (ylo // 2)))
        push_v(vslot(0, 2), 2, 2, 0, at_y(2 - 4 * (ylo // 2)))

    work_on((0, 1), (0, 3), between=far_on)
    pass_on(1)
    work_on((2, 0), (0, 2))
    work_on((1, 1), (1, 3), between=lambda: pass_on(3))
    take((2, 2))
    work_on((3, 1), (3, 3), between=lambda: take((2, 1), (2, 3)))
    take((1, 2))
    group, last = ((2, 1), (2, 3), (2, 2)), ((1, 2), (3, 2))
    ready(*group)
    work(group, (1,))
    take((3, 2))
    for copy in weights:
        copy.wait_recv()
    across_rows = [wbuf.at[pl.ds(d * HEAD + half_rows, HEAD // 2)] for d in range(1, NZ)]
    shared = [push(rows, rows, sibling) for rows in across_rows]
    ready(*last)

    given = []
    lane = lax.broadcasted_iota(jnp.int32, (STAT, HEAD), 1)

    def hand_over(side, block):
        if side == 0:
            return
        for part in range(block * ROWS // STAT, (block + 1) * ROWS // STAT):
            at, rows = pl.ds(TOK + part * STAT, STAT), pl.ds(part * STAT, STAT)
            give[rows, :] = acc[at, :HEAD].astype(jnp.bfloat16)
            give_stat[part] = jnp.where(lane == 0, peak[at, :], acc[at, HEAD:]).T[:8, :]
            given.append(
                (
                    push(give.at[rows], got.at[rows], at_y(toward)),
                    push(give_stat.at[part], got_stat.at[part], at_y(toward)),
                )
            )

    work(last, (1,), after=hand_over)
    work(group + last, (0,))

    rings = {}

    def rows_of(cut):
        return pl.ds(cut * CUT, CUT)

    def at_cut(cut, d):
        return around.at[rows_of(cut), pl.ds(d * HEAD, HEAD)]

    def send_z(cut, src, d, hop):
        rings[cut, d] = push(at_cut(cut, src), at_cut(cut, d), at_z(hop))

    def combine(part):
        rows = pl.ds(part * STAT, STAT)
        for copy in given[part]:
            copy.wait_recv()
        stat = jnp.concatenate([got_stat[part], jnp.zeros((STAT - 8, HEAD), jnp.float32)], axis=0).T
        peak_two, sum_two = stat[:, 0:1], stat[:, 1:2]
        peak_one, sum_one = peak[rows, :], acc[rows, HEAD:]
        top = jnp.maximum(peak_one, peak_two)
        one, two = jnp.exp2(peak_one - top), jnp.exp2(peak_two - top)
        total = acc[rows, :HEAD] * one + got[rows, :].astype(jnp.float32) * two
        around[rows, pl.ds(0, HEAD)] = (total / (sum_one * one + sum_two * two)).astype(jnp.bfloat16)

    def begin(cut):
        if cut * CUT % STAT == 0:
            combine(cut * CUT // STAT)
        send_z(cut, 0, 1, 1)
        send_z(cut, 0, NZ - 1, -1)
        if cut in DIRECT:
            send_z(cut, 0, 2, 2)
            send_z(cut, 0, NZ - 2, -2)

    def onward(cut, stage):
        if cut in DIRECT:
            if stage == 1:
                rings[cut, 2].wait_recv()
                send_z(cut, 2, 3, 1)
                if cut % 2 == 0:
                    send_z(cut, 2, 4, 2)
                rings[cut, NZ - 2].wait_recv()
                send_z(cut, NZ - 2, NZ - 3, -1)
                if cut % 2 == 1:
                    send_z(cut, NZ - 2, 4, -2)
            return
        rings[cut, stage].wait_recv()
        if stage < 3 or cut % 2 == 0:
            send_z(cut, stage, stage + 1, 1)
        rings[cut, NZ - stage].wait_recv()
        if stage < 3 or cut % 2 == 1:
            send_z(cut, NZ - stage, NZ - stage - 1, -1)

    swaps = []

    def project(cut):
        for d in (1, 7, 3, 5) if cut in DIRECT else ():
            rings[cut, d].wait_recv()
        rings[cut, 4].wait_recv()
        rows = rows_of(cut)
        part = jnp.dot(around[rows, :], wbuf[...], preferred_element_type=jnp.float32)
        own_part[rows, :] = part[:, :OUT]
        swap[rows, :] = part[:, OUT:].astype(jnp.bfloat16)
        swaps.append(push(swap.at[rows], swapped.at[rows], opposite))

    for copy in shared:
        copy.wait_recv()
    settled = 0

    def settle(count):
        nonlocal settled
        for copy in started[settled:count]:
            copy.wait_send()
        settled = max(settled, count)

    before = len(started)
    for cut, stage in TURNS:
        if (cut, stage) == (0, 1):
            settle(before)
        if stage == 0:
            begin(cut)
        elif stage == 4:
            project(cut)
        else:
            onward(cut, stage)
    settle(len(started) - 1)
    for cut in range(CUTS):
        rows = rows_of(cut)
        swaps[cut].wait_recv()
        out[rows, :] = (own_part[rows, :] + swapped[rows, :].astype(jnp.float32)).astype(jnp.bfloat16)
    settle(len(started))


def local(queries, keys, values, out_weight, slot_span):
    vmem, anywhere = pl.BlockSpec(memory_space=pltpu.VMEM), pl.BlockSpec(memory_space=pl.ANY)
    return pl.pallas_call(
        kernel,
        out_shape=jax.ShapeDtypeStruct((TOK, OUT), jnp.bfloat16),
        in_specs=[pl.BlockSpec(memory_space=pltpu.SMEM)] + [anywhere] * 4,
        out_specs=vmem,
        scratch_shapes=[
            pltpu.VMEM((TOK, HEAD), jnp.bfloat16),
            pltpu.VMEM((TOK, 4 * HEAD), jnp.bfloat16),
            pltpu.VMEM((TOK, 4 * HEAD), jnp.bfloat16),
            pltpu.VMEM((HEAD, 2 * NZ * OUT), jnp.bfloat16),
            pltpu.VMEM((2 * TOK, HEAD), jnp.bfloat16),
            pltpu.VMEM((4, NX, 2, HALF, HEAD), jnp.bfloat16),
            pltpu.VMEM((4, NX, 2, HALF, 2 * HEAD), jnp.bfloat16),
            pltpu.VMEM((NZ * HEAD, 2 * OUT), jnp.bfloat16),
            pltpu.VMEM((2 * TOK, 2 * HEAD), jnp.float32),
            pltpu.VMEM((2 * TOK, HEAD), jnp.float32),
            pltpu.VMEM((TOK, NZ * HEAD), jnp.bfloat16),
            pltpu.VMEM((TOK, HEAD), jnp.bfloat16),
            pltpu.VMEM((TOK, HEAD), jnp.bfloat16),
            pltpu.VMEM((TOK // STAT, 8, STAT), jnp.float32),
            pltpu.VMEM((TOK // STAT, 8, STAT), jnp.float32),
            pltpu.VMEM((TOK, OUT), jnp.float32),
            pltpu.VMEM((TOK, OUT), jnp.bfloat16),
            pltpu.VMEM((TOK, OUT), jnp.bfloat16),
            pltpu.SemaphoreType.DMA((COPIES,)),
            pltpu.SemaphoreType.DMA((COPIES,)),
            pltpu.SemaphoreType.DMA((9,)),
        ],
        compiler_params=pltpu.CompilerParams(
            collective_id=0, has_side_effects=True, vmem_limit_bytes=56 * 2**20
        ),
        cost_estimate=pl.CostEstimate(flops=9 * 10**9, bytes_accessed=3 * 10**6, transcendentals=9 * 10**6),
        name="attend_and_project",
    )(slot_span, queries, keys, values, out_weight)


def solution(mesh):
    in_specs = (P("row", "col"), P("row", None), P("row", None), P("col", None), P())
    return jax.shard_map(local, mesh=mesh, in_specs=in_specs, out_specs=P("row", "col"), check_vma=False)
```
